768 devices in a mesh: section: 8 (over x, core), expert: 12 (over z), dp: 8 (over y).
Axes of the slice: x: 4, y: 8, z: 12, core: 2. Of those that a mesh axis runs over, the one named last changes fastest.
Arguments:
- out_grad: bfloat16 [8, 1536, 7168], P('section', ('expert', 'dp')), may hold values from -6 to 6
- expert_ids: int32 [8, 1536, 1], P('section', ('expert', 'dp')), may hold values from 0 to 11; in each aligned block of 16 rows (0 to 15, 16 to 31, ..., all dimensions but the last counted through in order) at most 2 rows name the same one
- gate_weight: float32 [8, 1536, 1], P('section', ('expert', 'dp')), may hold values from 0.1 to 1
- gate_pre: bfloat16 [8, 12, 192, 1024], P('section', 'expert'), may hold values from -6 to 6
- up_pre: bfloat16 [8, 12, 192, 1024], P('section', 'expert'), may hold values from -6 to 6
- w_gate: bfloat16 [12, 7168, 1024], P('expert', 'dp'), may hold values from -0.0625 to 0.0625
- w_up: bfloat16 [12, 7168, 1024], P('expert', 'dp'), may hold values from -0.0625 to 0.0625
- w_down: bfloat16 [12, 1024, 7168], P('expert', None, 'dp'), may hold values from -0.1875 to 0.1875
Outputs:
- handed: bfloat16 [8, 1536, 7168], P('section', ('expert', 'dp'))
- grad_down: bfloat16 [8, 12, 1024, 7168], P('section', 'expert', None, 'dp')
The draws below stay inside these ranges and needn't reach their ends.
Inputs may be any that keep to these rules, and one draw needn't show every extreme that they name: `expert_ids`: each token names 1 expert. Among the 16 tokens of one device no expert is named more than 2 times, and in every draw some device's tokens name some expert exactly 2 times.
All inputs are finite; a program needn't handle non-finite values.
Results may differ from the reference program's by a relative error of at most 0.013.
Values may be sent and summed in bfloat16 or wider, within the bound.
No kernel may reach another device: no remote copies, remote signals or barrier semaphores. Data moves between devices by JAX's collectives and lax.ppermute only.
A program may use at most 32 MiB of HBM per device.

```python
import math
import jax
import jax.numpy as jnp
import numpy as np
from jax import lax

D = 7168
FF = 1024
TOPK = 1
TOK_DEV = 16
EXPERTS = 12
CAP = 2
MICRO = 8
TOKENS = 1536
ROWS = 192
N_EXPERT = 12
N_DP = 8


def levels(key, shape, cuts, least, top_value):
    loudness = 1.0
    for dim, blocks in cuts:
        draws = jax.random.uniform(jax.random.fold_in(jax.random.fold_in(key, 6), dim), (blocks,), jnp.float32, least / len(cuts), top_value / len(cuts))
        loudness = loudness * jnp.repeat(jnp.exp(draws), shape[dim] // blocks).reshape((-1,) + (1,) * (len(shape) - 1 - dim))
    return loudness


def shared_out(stream_key, own, number, rows, number_of, top, most, lean):
    sequence = jax.random.permutation(stream_key, number_of)
    crowded, ordinary = portions_of(number_of, rows * top, most, lean, True), portions_of(number_of, rows * top, most, lean, False)
    places = jnp.arange(number_of)

    def named(tallies, turn):
        used = int((tallies > 0).sum())
        fixed = max(1, used // 4)
        passed = fixed + (places - fixed + turn * (used - fixed)) % max(1, number_of - fixed)
        return jnp.zeros((number_of,), jnp.int32).at[sequence[jnp.where(places < fixed, places, passed)]].set(jnp.asarray(tallies, jnp.int32))

    tallies = jnp.where(number % 4 == 0, named(crowded, number // 4), named(ordinary, number - number // 4 - 1))
    mixed = jax.random.permutation(jax.random.fold_in(own, 3), number_of)
    donor, sink = mixed[0:number_of // 2 * 2:2], mixed[1:number_of // 2 * 2:2]
    slack = jnp.minimum(tallies[donor] - 1, most - tallies[sink]) // 2
    slack = jnp.where((donor == sequence[0]) | (sink == sequence[0]) | (tallies[sink] == 0), 0, jnp.maximum(slack, 0))
    passed = jax.random.randint(jax.random.fold_in(own, 4), (number_of // 2,), 0, 1 << 20) % (slack + 1)
    tallies = tallies.at[donor].add(-passed).at[sink].add(passed)
    items = jnp.searchsorted(jnp.cumsum(tallies), jnp.arange(rows * top), side="right").astype(jnp.int32)
    grid = items.reshape(top, rows).T
    grid = grid[jax.random.permutation(jax.random.fold_in(own, 1), rows)]
    turn = jax.random.randint(jax.random.fold_in(own, 2), (rows, 1), 0, top)
    return jnp.take_along_axis(grid, (jnp.arange(top)[None, :] + turn) % top, axis=1)


def portions_of(amount, total, reach, skew, full):
    loads = [(1 << 20) // math.isqrt(grade ** skew) + 1 for grade in range(1, amount + 1)]
    largest = reach if full else min(reach, max(-(-total // amount), total * loads[0] // sum(loads)))
    least = 1 if total - largest >= amount - 1 else 0
    holding, surplus = [largest] + [least] * (amount - 1), total - largest - least * (amount - 1)
    while surplus > 0:
        movable = [i for i in range(1, amount) if holding[i] < largest] or [i for i in range(1, amount) if holding[i] < reach]
        mass, left = sum([loads[i] for i in movable]), surplus
        for i in movable:
            extra = min(reach - holding[i], max(1, left * loads[i] // mass), surplus)
            holding[i] = holding[i] + extra
            surplus = surplus - extra
    return np.array(holding)


def centred(own_key, shape, scale, reach, pieces=(), kind=jnp.bfloat16):
    gain = levels(own_key, shape, pieces, -0.22, 0.18) if pieces else 1.0
    entries = jax.random.normal(own_key, shape, jnp.float32) * scale * gain
    return jnp.minimum(jnp.maximum(entries, -reach), reach).astype(kind)


def setup_inputs(seed: int = 0) -> dict:
    arg_keys = jax.random.split(jax.random.key(seed), 9)
    out_grad = centred(arg_keys[0], (MICRO, TOKENS, D), 1.0, 6.0, ((0, 8), (1, 96)))
    expert_ids_keys = jax.random.split(jax.random.fold_in(arg_keys[1], 1), MICRO * TOKENS // TOK_DEV)
    expert_ids_turns = jax.random.permutation(jax.random.fold_in(arg_keys[1], 3), MICRO * TOKENS // TOK_DEV)
    expert_ids = jax.vmap(lambda own, number: shared_out(jax.random.fold_in(arg_keys[1], 2), own, number, TOK_DEV, EXPERTS, TOPK, CAP, 2))(expert_ids_keys, expert_ids_turns).reshape((MICRO, TOKENS, TOPK))
    gate_weight = jnp.clip(jnp.exp(math.log(1.0) - 2.3025851 * jax.random.uniform(arg_keys[2], (MICRO, TOKENS, TOPK), jnp.float32) ** levels(arg_keys[2], (MICRO, TOKENS, TOPK), ((0, 8), (1, 96)), -0.2, 0.2)), 0.1, 1.0)
    gate_pre = centred(arg_keys[3], (MICRO, EXPERTS, ROWS, FF), 1.0, 6.0, ((0, 8), (1, 12)))
    up_pre = centred(arg_keys[4], (MICRO, EXPERTS, ROWS, FF), 1.0, 6.0, ((0, 8), (1, 12)))
    w_gate = centred(arg_keys[5], (EXPERTS, D, FF), D ** -0.5, 0.0625, ((0, 12), (1, 8)))
    w_up = centred(arg_keys[6], (EXPERTS, D, FF), D ** -0.5, 0.0625, ((0, 12), (1, 8)))
    w_down = centred(arg_keys[7], (EXPERTS, FF, D), FF ** -0.5, 0.1875, ((0, 12), (2, 8)))
    return dict(out_grad=out_grad, expert_ids=expert_ids, gate_weight=gate_weight, gate_pre=gate_pre, up_pre=up_pre, w_gate=w_gate, w_up=w_up, w_down=w_down)


def slot_numbers(ids, count):
    flat = ids.reshape(-1)
    onehot = (flat[:, None] == jnp.arange(count, dtype=jnp.int32)[None, :]).astype(jnp.int32)
    before = jnp.cumsum(onehot, axis=0) - onehot
    return jnp.sum(before * onehot, axis=1).reshape(ids.shape).astype(jnp.int32)


def hidden_partial(routed, weight_down):
    span = D // N_DP
    total = jnp.zeros((routed.shape[0], FF), jnp.float32)
    for part in range(N_DP):
        piece = jnp.dot(routed[:, part * span:(part + 1) * span], weight_down[:, part * span:(part + 1) * span].T, preferred_element_type=jnp.float32)
        rounded = lax.optimization_barrier(piece.astype(jnp.bfloat16))
        total = total + rounded.astype(jnp.float32)
    return total


def expert_step(items):
    routed, gate_in, up_in, weight_gate, weight_up, weight_down = items
    partial_value = hidden_partial(routed, weight_down)
    gvalue = gate_in.astype(jnp.float32)
    uvalue = up_in.astype(jnp.float32)
    sigma = jax.nn.sigmoid(gvalue)
    active = gvalue * sigma
    hidden = (active * uvalue).astype(jnp.bfloat16)
    down_grad = jnp.dot(hidden.T, routed, preferred_element_type=jnp.float32).astype(jnp.bfloat16)
    gate_grad = (partial_value * uvalue * sigma * (1.0 + gvalue * (1.0 - sigma))).astype(jnp.bfloat16)
    up_grad = (partial_value * active).astype(jnp.bfloat16)
    back = jnp.dot(gate_grad, weight_gate.T, preferred_element_type=jnp.float32)
    back = back + jnp.dot(up_grad, weight_up.T, preferred_element_type=jnp.float32)
    return back.astype(jnp.bfloat16), down_grad


def reference(out_grad, expert_ids, gate_weight, gate_pre, up_pre, w_gate, w_up, w_down):
    blocks = N_EXPERT * N_DP
    results = []
    grads = []
    for micro in range(MICRO):
        ids = expert_ids[micro].reshape(blocks, TOK_DEV, TOPK)
        slots = jax.vmap(lambda part: slot_numbers(part, EXPERTS))(ids)
        target = (ids * CAP + slots).astype(jnp.int32)
        grad = out_grad[micro].reshape(blocks, TOK_DEV, D)
        where = jnp.arange(blocks, dtype=jnp.int32)[:, None, None]
        values = jnp.broadcast_to(grad[:, :, None, :], (blocks, TOK_DEV, TOPK, D))
        buffer = jnp.zeros((blocks, EXPERTS * CAP, D), jnp.bfloat16).at[where, target].set(values)
        routed = buffer.reshape(N_EXPERT, N_DP, EXPERTS, CAP, D).transpose(2, 1, 0, 3, 4).reshape(EXPERTS, ROWS, D)
        back, down_grad = lax.map(expert_step, (routed, gate_pre[micro], up_pre[micro], w_gate, w_up, w_down))
        returned = back.reshape(EXPERTS, N_DP, N_EXPERT, CAP, D).transpose(2, 1, 0, 3, 4).reshape(blocks, EXPERTS * CAP, D)
        picked = returned[where, target].astype(jnp.float32)
        weights = gate_weight[micro].reshape(blocks, TOK_DEV, TOPK)
        total = grad.astype(jnp.float32) + jnp.sum(weights[..., None] * picked, axis=2)
        results.append(total.astype(jnp.bfloat16).reshape(TOKENS, D))
        grads.append(down_grad)
    handed = jnp.roll(jnp.stack(results), -1, axis=0)
    return handed, jnp.stack(grads)
```

```python
import jax
import jax.numpy as jnp
from jax import lax
from jax.sharding import PartitionSpec as P


def shifted(value, axis, steps):
    count = lax.axis_size(axis)
    pairs = [(source, (source + steps) % count) for source in range(count)]
    return lax.ppermute(value, axis, pairs)


def exchange(value, axes):
    return lax.all_to_all(value, axes, split_axis=0, concat_axis=0, tiled=True)


def slot_numbers(ids, count):
    flat = ids.reshape(-1)
    onehot = (flat[:, None] == jnp.arange(count, dtype=jnp.int32)[None, :]).astype(jnp.int32)
    before = jnp.cumsum(onehot, axis=0) - onehot
    return jnp.sum(before * onehot, axis=1).reshape(ids.shape)


def on_device(out_grad, expert_ids, gate_weight, gate_pre, up_pre, w_gate, w_up, w_down):
    n_expert = lax.axis_size("expert")
    n_replica = lax.axis_size("dp")
    grad = out_grad[0]
    ids = expert_ids[0]
    tok_count = grad.shape[0]
    width = grad.shape[1]
    rows = gate_pre.shape[2]
    hidden_width = gate_pre.shape[3]
    slots_per = rows // (n_replica * n_expert)
    slab = width // n_replica
    n_slots = n_expert * slots_per
    target = ids * slots_per + slot_numbers(ids, n_expert)
    places = target.reshape(-1)[None, :] == jnp.arange(n_slots, dtype=jnp.int32)[:, None]
    dispatch = places.astype(jnp.bfloat16)
    send = jnp.dot(dispatch, grad, preferred_element_type=jnp.float32).astype(jnp.bfloat16)
    send = send.reshape(n_expert, slots_per, n_replica, slab).transpose(2, 0, 1, 3)
    send = send.reshape(n_replica * n_expert, slots_per, slab)
    routed = exchange(send, ("dp", "expert")).reshape(rows, slab)
    partial_value = lax.dot_general(
        routed, w_down[0], (((1,), (1,)), ((), ())), preferred_element_type=jnp.float32
    ).astype(jnp.bfloat16)
    per = rows // n_replica
    parts = exchange(partial_value.reshape(n_replica, per, hidden_width), "dp")
    own = jnp.sum(parts.astype(jnp.float32), axis=0).astype(jnp.bfloat16)
    spread = jnp.broadcast_to(own[None], (n_replica, per, hidden_width))
    summed = exchange(spread, "dp").reshape(rows, hidden_width).astype(jnp.float32)

    gvalue = gate_pre[0, 0].astype(jnp.float32)
    uvalue = up_pre[0, 0].astype(jnp.float32)
    sigma = jax.nn.sigmoid(gvalue)
    hidden = (gvalue * sigma * uvalue).astype(jnp.bfloat16)
    down_grad = lax.dot_general(
        hidden, routed, (((0,), (0,)), ((), ())), preferred_element_type=jnp.float32
    )
    gate_grad = (summed * uvalue * sigma * (1.0 + gvalue * (1.0 - sigma))).astype(jnp.bfloat16)
    up_grad = (summed * gvalue * sigma).astype(jnp.bfloat16)
    back = lax.dot_general(
        gate_grad, w_gate[0], (((1,), (1,)), ((), ())), preferred_element_type=jnp.float32
    )
    back = back + lax.dot_general(
        up_grad, w_up[0], (((1,), (1,)), ((), ())), preferred_element_type=jnp.float32
    )
    back = back.astype(jnp.bfloat16).reshape(n_replica * n_expert, slots_per, slab)
    returned = exchange(back, ("dp", "expert"))
    returned = returned.reshape(n_replica, n_slots, slab)
    picked = jnp.einsum(
        "st,dsf->tdf", dispatch, returned, preferred_element_type=jnp.float32
    ).reshape(tok_count, width)
    total = grad.astype(jnp.float32) + gate_weight[0] * picked
    handed = shifted(total.astype(jnp.bfloat16), "section", -1)
    return (handed[None], down_grad.astype(jnp.bfloat16)[None, None])


def solution(mesh):
    placed = (
        P("section", ("expert", "dp"), None),
        P("section", ("expert", "dp"), None),
        P("section", ("expert", "dp"), None),
        P("section", "expert", None, None),
        P("section", "expert", None, None),
        P("expert", "dp", None),
        P("expert", "dp", None),
        P("expert", None, "dp"),
    )
    return jax.shard_map(
        on_device,
        mesh=mesh,
        in_specs=placed,
        out_specs=(P("section", ("expert", "dp"), None), P("section", "expert", None, "dp")),
        check_vma=False,
    )
```

```python
import functools

import jax
import jax.numpy as jnp
from jax import lax
from jax.experimental import pallas as pl
from jax.experimental.pallas import tpu as pltpu
from jax.sharding import PartitionSpec as P

F32 = jnp.float32
BF16 = jnp.bfloat16


def shifted(value, axis, steps):
    count = lax.axis_size(axis)
    pairs = [(source, (source + steps) % count) for source in range(count)]
    return lax.ppermute(value, axis, pairs)


def exchange(value, axes):
    return lax.all_to_all(value, axes, split_axis=0, concat_axis=0, tiled=True)


def dispatch_kernel(slots_per, ids_ref, grad_ref, send_ref, places_ref):
    tokens = ids_ref.shape[1]
    slots = places_ref.shape[0]
    blocks, _, slab = send_ref.shape
    experts = slots // slots_per
    ids = ids_ref[...].astype(F32)
    across = jnp.broadcast_to(ids, (tokens, tokens))
    row = lax.broadcasted_iota(jnp.int32, (tokens, tokens), 0)
    col = lax.broadcasted_iota(jnp.int32, (tokens, tokens), 1)
    down = jnp.sum(jnp.where(row == col, across, 0.0), axis=1, keepdims=True)
    earlier = jnp.where((down == across) & (row < col), 1.0, 0.0)
    target = ids * slots_per + jnp.sum(earlier, axis=0, keepdims=True)
    slot = lax.broadcasted_iota(jnp.int32, (slots, tokens), 0).astype(F32)
    places = jnp.where(slot == target, 1.0, 0.0).astype(BF16)
    places_ref[...] = places
    for part in range(blocks // experts):
        piece = grad_ref[:, part * slab : (part + 1) * slab]
        moved = jnp.dot(places, piece, preferred_element_type=F32).astype(BF16)
        send_ref[part * experts : (part + 1) * experts] = moved.reshape(experts, slots_per, slab)


def add_kernel(parts_ref, out_ref):
    replicas = parts_ref.shape[0]
    total = parts_ref[0].astype(F32)
    for part in range(1, replicas):
        total = total + parts_ref[part].astype(F32)
    own = total.astype(BF16)
    for part in range(replicas):
        out_ref[part] = own


def back_kernel(h_ref, gate_ref, up_ref, wg_ref, wu_ref, out_ref, gate_grad, up_grad):
    rows, slab = gate_ref.shape[0], wg_ref.shape[0]
    blocks, slots_per, _ = out_ref.shape

    def chunk(index, carry):
        part = pl.ds(pl.multiple_of(index * 16, 16), 16)
        h = h_ref[part].astype(F32)
        g = gate_ref[part].astype(F32)
        u = up_ref[part].astype(F32)
        s = 1.0 / (1.0 + jnp.exp(-g))
        hs = h * s
        gate_grad[part] = (hs * u * (1.0 + g * (1.0 - s))).astype(BF16)
        up_grad[part] = (hs * g).astype(BF16)
        return carry

    lax.fori_loop(0, rows // 16, chunk, 0)
    dims = (((1,), (1,)), ((), ()))
    step = 256
    for start in range(0, slab, step):
        cols = slice(start, min(start + step, slab))
        value = lax.dot_general(gate_grad[...], wg_ref[cols, :], dims, preferred_element_type=F32)
        value = value + lax.dot_general(up_grad[...], wu_ref[cols, :], dims, preferred_element_type=F32)
        out_ref[:, :, cols] = value.astype(BF16).reshape(blocks, slots_per, cols.stop - cols.start)


def final_kernel(recv_ref, places_ref, weight_ref, grad_ref, out_ref):
    slots, tokens = places_ref.shape
    blocks, slots_per, slab = recv_ref.shape
    experts = slots // slots_per
    across = jnp.broadcast_to(weight_ref[...], (tokens, tokens))
    row = lax.broadcasted_iota(jnp.int32, (tokens, tokens), 0)
    col = lax.broadcasted_iota(jnp.int32, (tokens, tokens), 1)
    weight = jnp.sum(jnp.where(row == col, across, 0.0), axis=1, keepdims=True)
    dims = (((0,), (0,)), ((), ()))
    for part in range(blocks // experts):
        piece = recv_ref[part * experts : (part + 1) * experts].reshape(slots, slab)
        picked = lax.dot_general(places_ref[...], piece, dims, preferred_element_type=F32)
        cols = slice(part * slab, (part + 1) * slab)
        out_ref[:, cols] = (grad_ref[:, cols].astype(F32) + weight * picked).astype(BF16)


VM = pl.BlockSpec(memory_space=pltpu.VMEM)
ANY = pl.BlockSpec(memory_space=pl.ANY)


def limit(mebibytes):
    return pltpu.CompilerParams(vmem_limit_bytes=mebibytes << 20)


def on_device(out_grad, expert_ids, gate_weight, gate_pre, up_pre, w_gate, w_up, w_down):
    n_expert = lax.axis_size("expert")
    n_replica = lax.axis_size("dp")
    grad = out_grad[0]
    tok_count = grad.shape[0]
    width = grad.shape[1]
    rows = gate_pre.shape[2]
    hidden_width = gate_pre.shape[3]
    slots_per = rows // (n_replica * n_expert)
    slab = width // n_replica
    n_slots = n_expert * slots_per
    send, places = pl.pallas_call(
        functools.partial(dispatch_kernel, slots_per),
        out_shape=(
            jax.ShapeDtypeStruct((n_replica * n_expert, slots_per, slab), BF16),
            jax.ShapeDtypeStruct((n_slots, tok_count), BF16),
        ),
        in_specs=[VM, VM],
        out_specs=(VM, VM),
        compiler_params=limit(4),
        name="dispatch",
    )(expert_ids.reshape(1, tok_count), grad)
    routed = exchange(send, ("dp", "expert"))
    routed = routed.reshape(rows, slab)
    partial_value = lax.dot_general(
        routed, w_down[0], (((1,), (1,)), ((), ())), preferred_element_type=F32
    ).astype(BF16)
    per = rows // n_replica
    spread = jax.ShapeDtypeStruct((n_replica, per, hidden_width), BF16)
    partial_value = partial_value.reshape(n_replica, per, hidden_width)
    parts = exchange(partial_value, "dp")
    summed = pl.pallas_call(
        add_kernel,
        out_shape=spread,
        in_specs=[VM],
        out_specs=VM,
        compiler_params=limit(2),
        name="add",
    )(parts)
    summed = exchange(summed, "dp").reshape(rows, hidden_width)
    saved = pltpu.VMEM((rows, hidden_width), BF16)
    back = pl.pallas_call(
        back_kernel,
        out_shape=jax.ShapeDtypeStruct((n_replica * n_expert, slots_per, slab), BF16),
        in_specs=[VM] * 5,
        out_specs=VM,
        scratch_shapes=[saved, saved],
        compiler_params=limit(6),
        name="back",
    )(summed, gate_pre[0, 0], up_pre[0, 0], w_gate[0], w_up[0])
    returned = exchange(back, ("dp", "expert"))
    total = pl.pallas_call(
        final_kernel,
        out_shape=jax.ShapeDtypeStruct((tok_count, width), BF16),
        in_specs=[VM] * 4,
        out_specs=VM,
        compiler_params=limit(4),
        name="final",
    )(returned, places, gate_weight.reshape(1, tok_count), grad)
    handed = shifted(total, "section", -1)
    gvalue = gate_pre[0, 0].astype(F32)
    act = (gvalue * jax.nn.sigmoid(gvalue) * up_pre[0, 0].astype(F32)).astype(BF16)
    down_grad = lax.dot_general(act, routed, (((0,), (0,)), ((), ())), preferred_element_type=F32)
    return (handed[None], down_grad.astype(BF16)[None, None])


def solution(mesh):
    placed = (
        P("section", ("expert", "dp"), None),
        P("section", ("expert", "dp"), None),
        P("section", ("expert", "dp"), None),
        P("section", "expert", None, None),
        P("section", "expert", None, None),
        P("expert", "dp", None),
        P("expert", "dp", None),
        P("expert", None, "dp"),
    )
    return jax.shard_map(
        on_device,
        mesh=mesh,
        in_specs=placed,
        out_specs=(P("section", ("expert", "dp"), None), P("section", "expert", None, "dp")),
        check_vma=False,
    )
```

```python
import functools

import jax
import jax.numpy as jnp
from jax import lax
from jax.experimental import pallas as pl
from jax.experimental.pallas import tpu as pltpu
from jax.sharding import PartitionSpec as P

F32 = jnp.float32
BF16 = jnp.bfloat16


def shifted(value, axis, steps):
    count = lax.axis_size(axis)
    pairs = [(source, (source + steps) % count) for source in range(count)]
    return lax.ppermute(value, axis, pairs)


def exchange(value, axes):
    return lax.all_to_all(value, axes, split_axis=0, concat_axis=0, tiled=True)


def dispatch_kernel(slots_per, ids_ref, grad_ref, send_ref, places_ref):
    tokens = ids_ref.shape[1]
    slots = places_ref.shape[0]
    blocks, _, slab = send_ref.shape
    experts = slots // slots_per
    ids = ids_ref[...].astype(F32)
    across = jnp.broadcast_to(ids, (tokens, tokens))
    row = lax.broadcasted_iota(jnp.int32, (tokens, tokens), 0)
    col = lax.broadcasted_iota(jnp.int32, (tokens, tokens), 1)
    down = jnp.sum(jnp.where(row == col, across, 0.0), axis=1, keepdims=True)
    earlier = jnp.where((down == across) & (row < col), 1.0, 0.0)
    target = ids * slots_per + jnp.sum(earlier, axis=0, keepdims=True)
    slot = lax.broadcasted_iota(jnp.int32, (slots, tokens), 0).astype(F32)
    places = jnp.where(slot == target, 1.0, 0.0).astype(BF16)
    places_ref[...] = places
    for part in range(blocks // experts):
        piece = grad_ref[:, part * slab : (part + 1) * slab]
        moved = jnp.dot(places, piece, preferred_element_type=F32).astype(BF16)
        send_ref[part * experts : (part + 1) * experts] = moved.reshape(experts, slots_per, slab)


def add_kernel(parts_ref, out_ref):
    replicas = parts_ref.shape[0]
    total = parts_ref[0].astype(F32)
    for part in range(1, replicas):
        total = total + parts_ref[part].astype(F32)
    own = total.astype(BF16)
    for part in range(replicas):
        out_ref[part] = own


def back_kernel(h_ref, gate_ref, up_ref, wg_ref, wu_ref, out_ref, gate_grad, up_grad):
    rows, slab = gate_ref.shape[0], wg_ref.shape[0]
    blocks, slots_per, _ = out_ref.shape

    def chunk(index, carry):
        part = pl.ds(pl.multiple_of(index * 16, 16), 16)
        h = h_ref[part].astype(F32)
        g = gate_ref[part].astype(F32)
        u = up_ref[part].astype(F32)
        s = 1.0 / (1.0 + jnp.exp(-g))
        hs = h * s
        gate_grad[part] = (hs * u * (1.0 + g * (1.0 - s))).astype(BF16)
        up_grad[part] = (hs * g).astype(BF16)
        return carry

    lax.fori_loop(0, rows // 16, chunk, 0, unroll=True)
    dims = (((1,), (1,)), ((), ()))
    step = 896
    for start in range(0, slab, step):
        cols = slice(start, min(start + step, slab))
        value = lax.dot_general(gate_grad[...], wg_ref[cols, :], dims, preferred_element_type=F32)
        value = value + lax.dot_general(up_grad[...], wu_ref[cols, :], dims, preferred_element_type=F32)
        out_ref[:, :, cols] = value.astype(BF16).reshape(blocks, slots_per, cols.stop - cols.start)


def final_kernel(recv_ref, places_ref, weight_ref, grad_ref, out_ref):
    slots, tokens = places_ref.shape
    blocks, slots_per, slab = recv_ref.shape
    experts = slots // slots_per
    across = jnp.broadcast_to(weight_ref[...], (tokens, tokens))
    row = lax.broadcasted_iota(jnp.int32, (tokens, tokens), 0)
    col = lax.broadcasted_iota(jnp.int32, (tokens, tokens), 1)
    weight = jnp.sum(jnp.where(row == col, across, 0.0), axis=1, keepdims=True)
    dims = (((0,), (0,)), ((), ()))
    for part in range(blocks // experts):
        piece = recv_ref[part * experts : (part + 1) * experts].reshape(slots, slab)
        picked = lax.dot_general(places_ref[...], piece, dims, preferred_element_type=F32)
        cols = slice(part * slab, (part + 1) * slab)
        out_ref[:, cols] = (grad_ref[:, cols].astype(F32) + weight * picked).astype(BF16)


VM = pl.BlockSpec(memory_space=pltpu.VMEM)
ANY = pl.BlockSpec(memory_space=pl.ANY)


def limit(mebibytes):
    return pltpu.CompilerParams(vmem_limit_bytes=mebibytes << 20)


def on_device(out_grad, expert_ids, gate_weight, gate_pre, up_pre, w_gate, w_up, w_down):
    n_expert = lax.axis_size("expert")
    n_replica = lax.axis_size("dp")
    grad = out_grad[0]
    tok_count = grad.shape[0]
    width = grad.shape[1]
    rows = gate_pre.shape[2]
    hidden_width = gate_pre.shape[3]
    slots_per = rows // (n_replica * n_expert)
    slab = width // n_replica
    n_slots = n_expert * slots_per
    send, places = pl.pallas_call(
        functools.partial(dispatch_kernel, slots_per),
        out_shape=(
            jax.ShapeDtypeStruct((n_replica * n_expert, slots_per, slab), BF16),
            jax.ShapeDtypeStruct((n_slots, tok_count), BF16),
        ),
        in_specs=[VM, VM],
        out_specs=(VM, VM),
        compiler_params=limit(4),
        name="dispatch",
    )(expert_ids.reshape(1, tok_count), grad)
    routed = exchange(send, ("dp", "expert"))
    routed = routed.reshape(rows, slab)
    partial_value = lax.dot_general(
        routed, w_down[0], (((1,), (1,)), ((), ())), preferred_element_type=F32
    ).astype(BF16)
    per = rows // n_replica
    spread = jax.ShapeDtypeStruct((n_replica, per, hidden_width), BF16)
    partial_value = partial_value.reshape(n_replica, per, hidden_width)
    parts = exchange(partial_value, "dp")
    summed = pl.pallas_call(
        add_kernel,
        out_shape=spread,
        in_specs=[VM],
        out_specs=VM,
        compiler_params=limit(2),
        name="add",
    )(parts)
    summed = exchange(summed, "dp").reshape(rows, hidden_width)
    saved = pltpu.VMEM((rows, hidden_width), BF16)
    back = pl.pallas_call(
        back_kernel,
        out_shape=jax.ShapeDtypeStruct((n_replica * n_expert, slots_per, slab), BF16),
        in_specs=[VM] * 5,
        out_specs=VM,
        scratch_shapes=[saved, saved],
        compiler_params=limit(6),
        name="back",
    )(summed, gate_pre[0, 0], up_pre[0, 0], w_gate[0], w_up[0])
    returned = exchange(back, ("dp", "expert"))
    total = pl.pallas_call(
        final_kernel,
        out_shape=jax.ShapeDtypeStruct((tok_count, width), BF16),
        in_specs=[VM] * 4,
        out_specs=VM,
        compiler_params=limit(4),
        name="final",
    )(returned, places, gate_weight.reshape(1, tok_count), grad)
    handed = shifted(total, "section", -1)
    gvalue = gate_pre[0, 0].astype(F32)
    act = (gvalue * jax.nn.sigmoid(gvalue) * up_pre[0, 0].astype(F32)).astype(BF16)
    down_grad = lax.dot_general(act, routed, (((0,), (0,)), ((), ())), preferred_element_type=F32)
    return (handed[None], down_grad.astype(BF16)[None, None])


def solution(mesh):
    placed = (
        P("section", ("expert", "dp"), None),
        P("section", ("expert", "dp"), None),
        P("section", ("expert", "dp"), None),
        P("section", "expert", None, None),
        P("section", "expert", None, None),
        P("expert", "dp", None),
        P("expert", "dp", None),
        P("expert", None, "dp"),
    )
    return jax.shard_map(
        on_device,
        mesh=mesh,
        in_specs=placed,
        out_specs=(P("section", ("expert", "dp"), None), P("section", "expert", None, "dp")),
        check_vma=False,
    )
```

```python
import functools

import jax
import jax.numpy as jnp
from jax import lax
from jax.experimental import pallas as pl
from jax.experimental.pallas import tpu as pltpu
from jax.sharding import PartitionSpec as P

F32 = jnp.float32
BF16 = jnp.bfloat16


def shifted(value, axis, steps):
    count = lax.axis_size(axis)
    pairs = [(source, (source + steps) % count) for source in range(count)]
    return lax.ppermute(value, axis, pairs)


def turn_token():
    sections, replicas = lax.axis_size("section"), lax.axis_size("dp")
    pairs = [
        (s * replicas + d, s * replicas + (d + 1) % replicas)
        for s in range(0, sections, 2)
        for d in range(replicas)
    ]
    return lax.ppermute(jnp.zeros((8, 128), F32), ("section", "dp"), pairs)


def turn_kernel(value_ref, turn_ref, out_ref):
    del value_ref, turn_ref, out_ref


def in_turn(value, token):
    return pl.pallas_call(
        turn_kernel,
        out_shape=jax.ShapeDtypeStruct(value.shape, value.dtype),
        in_specs=[VM, VM],
        out_specs=VM,
        input_output_aliases={0: 0},
        compiler_params=limit(2),
        name="turn",
    )(value, token)


def exchange(value, axes):
    return lax.all_to_all(value, axes, split_axis=0, concat_axis=0, tiled=True)


def dispatch_kernel(slots_per, ids_ref, grad_ref, send_ref, places_ref):
    tokens = ids_ref.shape[1]
    slots = places_ref.shape[0]
    blocks, _, slab = send_ref.shape
    experts = slots // slots_per
    ids = ids_ref[...].astype(F32)
    across = jnp.broadcast_to(ids, (tokens, tokens))
    row = lax.broadcasted_iota(jnp.int32, (tokens, tokens), 0)
    col = lax.broadcasted_iota(jnp.int32, (tokens, tokens), 1)
    down = jnp.sum(jnp.where(row == col, across, 0.0), axis=1, keepdims=True)
    earlier = jnp.where((down == across) & (row < col), 1.0, 0.0)
    target = ids * slots_per + jnp.sum(earlier, axis=0, keepdims=True)
    slot = lax.broadcasted_iota(jnp.int32, (slots, tokens), 0).astype(F32)
    places = jnp.where(slot == target, 1.0, 0.0).astype(BF16)
    places_ref[...] = places
    for part in range(blocks // experts):
        piece = grad_ref[:, part * slab : (part + 1) * slab]
        moved = jnp.dot(places, piece, preferred_element_type=F32).astype(BF16)
        send_ref[part * experts : (part + 1) * experts] = moved.reshape(experts, slots_per, slab)


def add_kernel(parts_ref, out_ref):
    replicas = parts_ref.shape[0]
    total = parts_ref[0].astype(F32)
    for part in range(1, replicas):
        total = total + parts_ref[part].astype(F32)
    own = total.astype(BF16)
    for part in range(replicas):
        out_ref[part] = own


def back_kernel(h_ref, gate_ref, up_ref, wg_ref, wu_ref, out_ref, gate_grad, up_grad):
    rows, slab = gate_ref.shape[0], wg_ref.shape[0]
    blocks, slots_per, _ = out_ref.shape

    def chunk(index, carry):
        part = pl.ds(pl.multiple_of(index * 16, 16), 16)
        h = h_ref[part].astype(F32)
        g = gate_ref[part].astype(F32)
        u = up_ref[part].astype(F32)
        s = 1.0 / (1.0 + jnp.exp(-g))
        hs = h * s
        gate_grad[part] = (hs * u * (1.0 + g * (1.0 - s))).astype(BF16)
        up_grad[part] = (hs * g).astype(BF16)
        return carry

    lax.fori_loop(0, rows // 16, chunk, 0, unroll=True)
    dims = (((1,), (1,)), ((), ()))
    step = 896
    for start in range(0, slab, step):
        cols = slice(start, min(start + step, slab))
        value = lax.dot_general(gate_grad[...], wg_ref[cols, :], dims, preferred_element_type=F32)
        value = value + lax.dot_general(up_grad[...], wu_ref[cols, :], dims, preferred_element_type=F32)
        out_ref[:, :, cols] = value.astype(BF16).reshape(blocks, slots_per, cols.stop - cols.start)


def final_kernel(recv_ref, places_ref, weight_ref, grad_ref, out_ref):
    slots, tokens = places_ref.shape
    blocks, slots_per, slab = recv_ref.shape
    experts = slots // slots_per
    across = jnp.broadcast_to(weight_ref[...], (tokens, tokens))
    row = lax.broadcasted_iota(jnp.int32, (tokens, tokens), 0)
    col = lax.broadcasted_iota(jnp.int32, (tokens, tokens), 1)
    weight = jnp.sum(jnp.where(row == col, across, 0.0), axis=1, keepdims=True)
    dims = (((0,), (0,)), ((), ()))
    for part in range(blocks // experts):
        piece = recv_ref[part * experts : (part + 1) * experts].reshape(slots, slab)
        picked = lax.dot_general(places_ref[...], piece, dims, preferred_element_type=F32)
        cols = slice(part * slab, (part + 1) * slab)
        out_ref[:, cols] = (grad_ref[:, cols].astype(F32) + weight * picked).astype(BF16)


VM = pl.BlockSpec(memory_space=pltpu.VMEM)
ANY = pl.BlockSpec(memory_space=pl.ANY)


def limit(mebibytes):
    return pltpu.CompilerParams(vmem_limit_bytes=mebibytes << 20)


def on_device(out_grad, expert_ids, gate_weight, gate_pre, up_pre, w_gate, w_up, w_down):
    n_expert = lax.axis_size("expert")
    n_replica = lax.axis_size("dp")
    grad = out_grad[0]
    tok_count = grad.shape[0]
    width = grad.shape[1]
    rows = gate_pre.shape[2]
    hidden_width = gate_pre.shape[3]
    slots_per = rows // (n_replica * n_expert)
    slab = width // n_replica
    n_slots = n_expert * slots_per
    send, places = pl.pallas_call(
        functools.partial(dispatch_kernel, slots_per),
        out_shape=(
            jax.ShapeDtypeStruct((n_replica * n_expert, slots_per, slab), BF16),
            jax.ShapeDtypeStruct((n_slots, tok_count), BF16),
        ),
        in_specs=[VM, VM],
        out_specs=(VM, VM),
        compiler_params=limit(4),
        name="dispatch",
    )(expert_ids.reshape(1, tok_count), grad)
    send = in_turn(send, turn_token())
    routed = exchange(send, ("dp", "expert"))
    routed = routed.reshape(rows, slab)
    partial_value = lax.dot_general(
        routed, w_down[0], (((1,), (1,)), ((), ())), preferred_element_type=F32
    ).astype(BF16)
    per = rows // n_replica
    spread = jax.ShapeDtypeStruct((n_replica, per, hidden_width), BF16)
    partial_value = partial_value.reshape(n_replica, per, hidden_width)
    parts = exchange(partial_value, "dp")
    summed = pl.pallas_call(
        add_kernel,
        out_shape=spread,
        in_specs=[VM],
        out_specs=VM,
        compiler_params=limit(2),
        name="add",
    )(parts)
    summed = exchange(summed, "dp").reshape(rows, hidden_width)
    saved = pltpu.VMEM((rows, hidden_width), BF16)
    back = pl.pallas_call(
        back_kernel,
        out_shape=jax.ShapeDtypeStruct((n_replica * n_expert, slots_per, slab), BF16),
        in_specs=[VM] * 5,
        out_specs=VM,
        scratch_shapes=[saved, saved],
        compiler_params=limit(6),
        name="back",
    )(summed, gate_pre[0, 0], up_pre[0, 0], w_gate[0], w_up[0])
    returned = exchange(back, ("dp", "expert"))
    total = pl.pallas_call(
        final_kernel,
        out_shape=jax.ShapeDtypeStruct((tok_count, width), BF16),
        in_specs=[VM] * 4,
        out_specs=VM,
        compiler_params=limit(4),
        name="final",
    )(returned, places, gate_weight.reshape(1, tok_count), grad)
    handed = shifted(total, "section", -1)
    gvalue = gate_pre[0, 0].astype(F32)
    act = (gvalue * jax.nn.sigmoid(gvalue) * up_pre[0, 0].astype(F32)).astype(BF16)
    down_grad = lax.dot_general(act, routed, (((0,), (0,)), ((), ())), preferred_element_type=F32)
    return (handed[None], down_grad.astype(BF16)[None, None])


def solution(mesh):
    placed = (
        P("section", ("expert", "dp"), None),
        P("section", ("expert", "dp"), None),
        P("section", ("expert", "dp"), None),
        P("section", "expert", None, None),
        P("section", "expert", None, None),
        P("expert", "dp", None),
        P("expert", "dp", None),
        P("expert", None, "dp"),
    )
    return jax.shard_map(
        on_device,
        mesh=mesh,
        in_specs=placed,
        out_specs=(P("section", ("expert", "dp"), None), P("section", "expert", None, "dp")),
        check_vma=False,
    )
```
